128 devices in a mesh: ctx: 32 (over z, y_hi, x), ch: 4 (over y_lo, core).
Axes of the slice: x: 4, y: 4 (y_hi: 2, y_lo: 2; y = y_hi * 2 + y_lo), z: 4, core: 2. Of those that a mesh axis runs over, the one named last changes fastest.
Arguments:
- features: bfloat16 [24576, 8192], P('ctx', 'ch'), may hold values from -6 to 6
- in_weight: bfloat16 [8192, 3, 1024], P(None, None, 'ch'), may hold values from -0.0625 to 0.0625
- filter_taps: bfloat16 [1536, 1024], P('ctx', 'ch'), may hold values from -0.15625 to 0.15625
Outputs:
- gated: bfloat16 [24576, 1024], P('ctx', 'ch')
The draws below stay inside these ranges and needn't reach their ends.
All inputs are finite; a program needn't handle non-finite values.
Results may differ from the reference program's by a relative error of at most 0.012.
Values may be sent and summed in bfloat16 or wider, within the bound.
No kernel may reach another device: no remote copies, remote signals or barrier semaphores. Data moves between devices by JAX's collectives and lax.ppermute only.
A program may use at most 128 MiB of HBM per device.

```python
import jax
import jax.numpy as jnp
from jax import lax

DM = 8192
D = 1024
TOKENS = 24576
LAG = 1536


def block_scale(key, extent, cuts, low, largest):
    def one(dim, shards_of):
        steps = jax.random.uniform(jax.random.fold_in(jax.random.fold_in(key, 6), dim), (shards_of,), jnp.float32, low / len(cuts), largest / len(cuts))
        return jnp.repeat(jnp.exp(steps), extent[dim] // shards_of).reshape((-1,) + (1,) * (len(extent) - dim - 1))

    gain = one(*cuts[0])
    for cut in cuts[1:]:
        gain = gain * one(*cut)
    return gain


def bell_draw(own_key, extent, deviation, limit, cuts=(), kind=jnp.bfloat16):
    entries = deviation * jax.random.normal(own_key, extent, jnp.float32)
    if cuts:
        entries = entries * block_scale(own_key, extent, cuts, -0.22, 0.18)
    return jnp.clip(entries, -limit, limit).astype(kind)


def setup_inputs(seed: int = 0) -> dict:
    seeds = jax.random.split(jax.random.key(seed), 4)
    return {
        "features": bell_draw(seeds[0], (TOKENS, DM), 1.0, 6.0, ((0, 32), (1, 4))),
        "in_weight": bell_draw(seeds[1], (DM, 3, D), DM ** -0.5, 0.0625, ((2, 4),)),
        "filter_taps": bell_draw(seeds[2], (LAG, D), LAG ** -0.5, 0.15625, ((0, 32), (1, 4))),
    }


def reference(features, in_weight, filter_taps):
    projected = jnp.dot(features, in_weight.reshape(DM, 3 * D), preferred_element_type=jnp.float32).reshape(TOKENS, 3, D)
    queries = projected[:, 0, :].astype(jnp.bfloat16)
    product = (projected[:, 1, :] * projected[:, 2, :]).astype(jnp.bfloat16)
    fft_size = 1 << (TOKENS + LAG - 1).bit_length()
    group_size = min(64, D)
    signal = product.astype(jnp.float32).T.reshape(D // group_size, group_size, TOKENS)
    kernel = filter_taps.astype(jnp.float32).T.reshape(D // group_size, group_size, LAG)

    def convolve_group(pair):
        spectrum = jnp.fft.rfft(pair[0], n=fft_size, axis=-1) * jnp.fft.rfft(pair[1], n=fft_size, axis=-1)
        return jnp.fft.irfft(spectrum, n=fft_size, axis=-1)[:, :TOKENS].astype(jnp.float32)

    convolved = lax.map(convolve_group, (signal, kernel)).reshape(D, TOKENS).T
    return (queries.astype(jnp.float32) * convolved).astype(jnp.bfloat16)
```

```python
import functools

import jax
import jax.numpy as jnp
import numpy as np
from jax import lax
from jax.experimental import pallas as pl
from jax.experimental.pallas import tpu as pltpu
from jax.sharding import PartitionSpec as P

BLOCK = 256
WHOLE = pl.BlockSpec(memory_space=pltpu.VMEM)
SCALAR = pl.BlockSpec(memory_space=pltpu.SMEM)
SMALL = pl.CostEstimate(flops=1024, bytes_accessed=1024, transcendentals=0)
CHUNKS = ((0, 256), (256, 256), (512, 128), (640, 128))
PEER = [(0, 2), (1, 3), (2, 0), (3, 1)]
SIBLING = [(0, 1), (1, 0), (2, 3), (3, 2)]


def spectral_tables():
    order = np.concatenate([np.arange(0, BLOCK, 2), np.arange(1, BLOCK, 2)])
    theta = np.pi * (2 * order + 1) / (2 * BLOCK)
    near = theta[:, None] * np.arange(BLOCK)[None, :]
    far = (np.arange(BLOCK) + BLOCK)[:, None] * theta[None, :]
    forward = np.concatenate([np.cos(near), np.sin(near)], 0)
    inverse = np.concatenate([np.cos(far), np.sin(far)], 1) / BLOCK
    return jnp.asarray(forward, jnp.bfloat16), jnp.asarray(inverse, jnp.bfloat16)


def weight_specs(depth, width, splits, first):
    return [
        pl.BlockSpec(
            (1, depth // splits, width),
            lambda s, o, kind=kind: (kind, o[first + s // splits] * splits + s % splits, 0),
        )
        for kind in range(3)
    ]


def project_own_kernel(order, own, sibling, *refs):
    weights, outs = refs[:3], refs[3:]
    step = pl.program_id(0)
    depth = weights[0].shape[1]
    splits = own.shape[1] // depth
    for turn in range(2 * splits):

        @pl.when(step == turn)
        def _():
            piece = (own, sibling)[turn // splits]
            columns = slice(turn % splits * depth, (turn % splits + 1) * depth)
            for kind, weight in enumerate(weights):
                at = 0
                for out in outs:
                    part = jnp.dot(
                        piece[at : at + out.shape[1], columns], weight[0], preferred_element_type=jnp.float32
                    )
                    out[kind] = part if turn == 0 else out[kind] + part
                    at += out.shape[1]


def project_own(order, features, sibling, weight):
    rows, depth = features.shape
    width = weight.shape[2]
    splits = 2
    alone = pl.BlockSpec((rows, depth), lambda s, o: (0, 0))
    return pl.pallas_call(
        project_own_kernel,
        out_shape=[jax.ShapeDtypeStruct((3, size, width), jnp.float32) for _, size in CHUNKS],
        grid_spec=pltpu.PrefetchScalarGridSpec(
            num_scalar_prefetch=1,
            grid=(2 * splits,),
            in_specs=[alone, alone] + weight_specs(depth, width, splits, 0),
            out_specs=[pl.BlockSpec((3, size, width), lambda s, o: (0, 0, 0)) for _, size in CHUNKS],
        ),
        compiler_params=pltpu.CompilerParams(vmem_limit_bytes=28 << 20),
        cost_estimate=SMALL,
        name="project_own",
    )(order, features, sibling, weight, weight, weight)


def project_peer_kernel(order, peer, peer_sibling, known, *refs):
    weights, (query, product, total) = refs[:3], refs[3:]
    step = pl.program_id(0)
    depth = weights[0].shape[1]
    splits = peer.shape[1] // depth
    for turn in range(2 * splits):

        @pl.when(step == turn)
        def _():
            piece = (peer, peer_sibling)[turn // splits]
            columns = slice(turn % splits * depth, (turn % splits + 1) * depth)
            full = []
            for kind, weight in enumerate(weights):
                part = jnp.dot(piece[:, columns], weight[0], preferred_element_type=jnp.float32)
                full.append(part + (known[kind] if turn == 0 else total[kind]))
            if turn < 2 * splits - 1:
                for kind in range(3):
                    total[kind] = full[kind]
            else:
                query[...] = full[0].astype(jnp.bfloat16)
                product[...] = (full[1] * full[2]).astype(jnp.bfloat16)


def project_peer(order, peer, peer_sibling, known, weight):
    rows, depth = peer.shape
    width = weight.shape[2]
    splits = 2
    alone = pl.BlockSpec((rows, depth), lambda s, o: (0, 0))
    out = pl.BlockSpec((rows, width), lambda s, o: (0, 0))
    return pl.pallas_call(
        project_peer_kernel,
        out_shape=[jax.ShapeDtypeStruct((rows, width), jnp.bfloat16)] * 2,
        grid_spec=pltpu.PrefetchScalarGridSpec(
            num_scalar_prefetch=1,
            grid=(2 * splits,),
            in_specs=[alone, alone, pl.BlockSpec((3, rows, width), lambda s, o: (0, 0, 0))]
            + weight_specs(depth, width, splits, 2),
            out_specs=[out, out],
            scratch_shapes=[pltpu.VMEM((3, rows, width), jnp.float32)],
        ),
        compiler_params=pltpu.CompilerParams(vmem_limit_bytes=16 << 20),
        cost_estimate=SMALL,
        name="project_peer",
    )(order, peer, peer_sibling, known, weight, weight, weight)


def taps_kernel(taps, forward, spectrum):
    for block in range(taps.shape[0] // BLOCK):
        spectrum[block] = jnp.dot(
            forward[...], taps[block * BLOCK : (block + 1) * BLOCK], preferred_element_type=jnp.float32
        )


def transform_taps(taps, forward):
    blocks, width = taps.shape[0] // BLOCK, taps.shape[1]
    return pl.pallas_call(
        taps_kernel,
        out_shape=jax.ShapeDtypeStruct((blocks, 2 * BLOCK, width), jnp.float32),
        compiler_params=pltpu.CompilerParams(vmem_limit_bytes=16 << 20),
        cost_estimate=SMALL,
        name="transform_taps",
    )(taps, forward)


def convolve_kernel(counts, *refs):
    n_source, n_query = counts
    sources = refs[:n_source]
    queries = refs[n_source : n_source + n_query]
    taps, forward, inverse, out, signal, spectrum, mixed = refs[n_source + n_query :]
    at = 0
    for source in sources:
        signal[at : at + source.shape[0]] = source[...]
        at += source.shape[0]
    n_blocks = at // BLOCK
    n_taps = taps.shape[0]
    n_out = n_blocks - n_taps
    for block in range(n_blocks):
        spectrum[block] = jnp.dot(
            forward[...], signal[block * BLOCK : (block + 1) * BLOCK], preferred_element_type=jnp.float32
        )
    half = BLOCK // 2
    rows = 8
    for sign in (0, 1):

        def mix(turn, carry):
            base = pl.multiple_of(sign * half + turn * rows, rows)
            cos_at = pl.ds(base, rows)
            sin_at = pl.ds(base + BLOCK, rows)
            pairs = []
            for pair in range(n_blocks - 1):
                near_cos, near_sin = spectrum[pair, cos_at], spectrum[pair, sin_at]
                far_cos, far_sin = spectrum[pair + 1, cos_at], spectrum[pair + 1, sin_at]
                if sign == 0:
                    pairs.append((near_cos - far_sin, near_sin + far_cos))
                else:
                    pairs.append((near_cos + far_sin, near_sin - far_cos))
            for j in range(n_out):
                cos_sum = sin_sum = None
                for i in range(n_taps):
                    c, s = pairs[n_taps - 1 + j - i]
                    hc, hs = taps[i, cos_at], taps[i, sin_at]
                    cc, ss = c * hc - s * hs, c * hs + s * hc
                    cos_sum = cc if cos_sum is None else cos_sum + cc
                    sin_sum = ss if sin_sum is None else sin_sum + ss
                mixed[j, cos_at] = cos_sum
                mixed[j, sin_at] = sin_sum
            return carry

        lax.fori_loop(0, half // rows, mix, 0)
    convolved = [
        jnp.dot(inverse[...], mixed[j].astype(jnp.bfloat16), preferred_element_type=jnp.float32) for j in range(n_out)
    ]
    at = 0
    for query in queries:
        for row in range(0, query.shape[0], 128):
            block, offset = (at + row) // BLOCK, (at + row) % BLOCK
            out[at + row : at + row + 128] = (
                query[row : row + 128].astype(jnp.float32) * convolved[block][offset : offset + 128]
            ).astype(jnp.bfloat16)
        at += query.shape[0]


def convolve(sources, queries, taps, forward, inverse):
    length = sum(s.shape[0] for s in sources)
    rows = sum(q.shape[0] for q in queries)
    width = queries[0].shape[1]
    blocks = length // BLOCK
    outs = rows // BLOCK
    return pl.pallas_call(
        functools.partial(convolve_kernel, (len(sources), len(queries))),
        out_shape=jax.ShapeDtypeStruct((rows, width), jnp.bfloat16),
        scratch_shapes=[
            pltpu.VMEM((length, width), jnp.bfloat16),
            pltpu.VMEM((blocks, 2 * BLOCK, width), jnp.float32),
            pltpu.VMEM((outs, 2 * BLOCK, width), jnp.float32),
        ],
        compiler_params=pltpu.CompilerParams(vmem_limit_bytes=20 << 20),
        cost_estimate=SMALL,
        name="convolve",
    )(*sources, *queries, taps, forward, inverse)


def pair_taps(taps):
    other = lax.ppermute(taps, "ctx", [(i, i ^ 4) for i in range(32)])
    upper = (lax.axis_index("ctx") & 4) != 0
    return jnp.where(upper, jnp.stack([other, taps]), jnp.stack([taps, other]))


def exchange_taps(both):
    _, lags, width = both.shape
    groups = [[z * 8 + y * 4 + x for z in range(4) for x in range(4)] for y in range(2)]
    copies = jnp.broadcast_to(both[None], (16, 2, lags, width))
    every = lax.all_to_all(copies, "ctx", 0, 0, axis_index_groups=groups, tiled=True)
    return every.reshape(4, 4, 2, lags, width).transpose(0, 2, 1, 3, 4).reshape(-1, width)


def body(features, in_weight, filter_taps):
    peers = lax.axis_size("ctx")
    ahead = [[(i, i + by) for i in range(peers - by)] for by in (1, 2)]
    me = lax.axis_index("ch")
    order = jnp.stack([me, me ^ 1, me ^ 2, me ^ 3]).astype(jnp.int32)
    weight = jnp.transpose(in_weight, (1, 0, 2))
    forward, inverse = spectral_tables()

    together = lax.optimization_barrier
    both = pair_taps(filter_taps)
    sibling = lax.ppermute(features, "ch", SIBLING)
    arrived = []
    for turn, (at, rows) in enumerate(CHUNKS):
        whole = features
        if turn == 1:
            whole, sibling = together((features, sibling))
        elif turn >= 2:
            whole, arrived[turn - 2] = together((features, arrived[turn - 2]))
        piece = whole[at : at + rows]
        if turn == 0:
            piece, both = together((piece, both))
        arrived.append(lax.ppermute(piece, "ch", PEER))
    taps = exchange_taps(both)
    known = list(project_own(order, features, sibling, weight))

    def send(group):
        return [lax.ppermute(group, "ctx", ahead[by]) for by in (0, 1)]

    def finish(turn, peer):
        peer_sibling = lax.ppermute(peer, "ch", SIBLING)
        return project_peer(order, peer, peer_sibling, known[turn], weight)

    peer, taps = together((arrived[0], taps))
    query_0, product_0 = finish(0, peer)
    halo_0 = send(product_0)
    peer, known[0], known[1] = together((arrived[1], known[0], known[1]))
    query_1, product_1 = finish(1, peer)
    spectrum = transform_taps(taps, forward)
    peer, product_0, halo_0[0], halo_0[1], spectrum = together(
        (arrived[2], product_0, halo_0[0], halo_0[1], spectrum)
    )
    query_2, product_2 = finish(2, peer)
    halo_1 = send(product_1)
    peer, product_1 = together((arrived[3], product_1))
    query_3, product_3 = finish(3, peer)
    halo_2 = send(jnp.concatenate([product_2, product_3], 0))
    sources = [halo_0[1], halo_1[1], halo_2[1], halo_0[0], halo_1[0], halo_2[0]]
    sources += [product_0, product_1, product_2, product_3]
    return convolve(sources, [query_0, query_1, query_2, query_3], spectrum, forward, inverse)


def solution(mesh):
    in_specs = (P("ctx", "ch"), P(None, None, "ch"), P("ctx", "ch"))
    out_specs = P("ctx", "ch")
    return jax.shard_map(body, mesh=mesh, in_specs=in_specs, out_specs=out_specs, check_vma=False)
```

```python
import functools

import jax
import jax.numpy as jnp
import numpy as np
from jax import lax
from jax.experimental import pallas as pl
from jax.experimental.pallas import tpu as pltpu
from jax.sharding import PartitionSpec as P

BLOCK = 256
WHOLE = pl.BlockSpec(memory_space=pltpu.VMEM)
SCALAR = pl.BlockSpec(memory_space=pltpu.SMEM)
SMALL = pl.CostEstimate(flops=1024, bytes_accessed=1024, transcendentals=0)
SIZES = (320, 384, 64)
CHUNKS = tuple((sum(SIZES[:turn]), size) for turn, size in enumerate(SIZES))
GROUPS = ((0, 1), (2,))
BEFORE_SEND = ((), ("sibling",), ("arrived0",))
BEFORE_PASS = (("taps",), ("product0", "spectrum"), ("product1",))
BEFORE_START = ("both",)
PEER = [(0, 2), (1, 3), (2, 0), (3, 1)]
SIBLING = [(0, 1), (1, 0), (2, 3), (3, 2)]


def spectral_tables():
    order = np.concatenate([np.arange(0, BLOCK, 2), np.arange(1, BLOCK, 2)])
    theta = np.pi * (2 * order + 1) / (2 * BLOCK)
    near = theta[:, None] * np.arange(BLOCK)[None, :]
    far = (np.arange(BLOCK) + BLOCK)[:, None] * theta[None, :]
    forward = np.concatenate([np.cos(near), np.sin(near)], 0)
    inverse = np.concatenate([np.cos(far), np.sin(far)], 1) / BLOCK
    return jnp.asarray(forward, jnp.bfloat16), jnp.asarray(inverse, jnp.bfloat16)


def weight_specs(depth, width, splits, first):
    return [
        pl.BlockSpec(
            (1, depth // splits, width),
            lambda s, o, kind=kind: (kind, o[first + s // splits] * splits + s % splits, 0),
        )
        for kind in range(3)
    ]


def project_own_kernel(order, own, sibling, *refs):
    weights, outs = refs[:3], refs[3:]
    step = pl.program_id(0)
    depth = weights[0].shape[1]
    splits = own.shape[1] // depth
    for turn in range(2 * splits):

        @pl.when(step == turn)
        def _():
            piece = (own, sibling)[turn // splits]
            columns = slice(turn % splits * depth, (turn % splits + 1) * depth)
            for kind, weight in enumerate(weights):
                at = 0
                for out in outs:
                    part = jnp.dot(
                        piece[at : at + out.shape[1], columns], weight[0], preferred_element_type=jnp.float32
                    )
                    out[kind] = part if turn == 0 else out[kind] + part
                    at += out.shape[1]


def project_own(order, features, sibling, weight):
    rows, depth = features.shape
    width = weight.shape[2]
    splits = 2
    alone = pl.BlockSpec((rows, depth), lambda s, o: (0, 0))
    return pl.pallas_call(
        project_own_kernel,
        out_shape=[jax.ShapeDtypeStruct((3, size, width), jnp.float32) for _, size in CHUNKS],
        grid_spec=pltpu.PrefetchScalarGridSpec(
            num_scalar_prefetch=1,
            grid=(2 * splits,),
            in_specs=[alone, alone] + weight_specs(depth, width, splits, 0),
            out_specs=[pl.BlockSpec((3, size, width), lambda s, o: (0, 0, 0)) for _, size in CHUNKS],
        ),
        compiler_params=pltpu.CompilerParams(vmem_limit_bytes=28 << 20),
        cost_estimate=SMALL,
        name="project_own",
    )(order, features, sibling, weight, weight, weight)


def project_peer_kernel(order, peer, peer_sibling, known, *refs):
    weights, (query, product, total) = refs[:3], refs[3:]
    step = pl.program_id(0)
    depth = weights[0].shape[1]
    splits = peer.shape[1] // depth
    for turn in range(2 * splits):

        @pl.when(step == turn)
        def _():
            piece = (peer, peer_sibling)[turn // splits]
            columns = slice(turn % splits * depth, (turn % splits + 1) * depth)
            full = []
            for kind, weight in enumerate(weights):
                part = jnp.dot(piece[:, columns], weight[0], preferred_element_type=jnp.float32)
                full.append(part + (known[kind] if turn == 0 else total[kind]))
            if turn < 2 * splits - 1:
                for kind in range(3):
                    total[kind] = full[kind]
            else:
                query[...] = full[0].astype(jnp.bfloat16)
                product[...] = (full[1] * full[2]).astype(jnp.bfloat16)


def project_peer(order, peer, peer_sibling, known, weight):
    rows, depth = peer.shape
    width = weight.shape[2]
    splits = 2
    alone = pl.BlockSpec((rows, depth), lambda s, o: (0, 0))
    out = pl.BlockSpec((rows, width), lambda s, o: (0, 0))
    return pl.pallas_call(
        project_peer_kernel,
        out_shape=[jax.ShapeDtypeStruct((rows, width), jnp.bfloat16)] * 2,
        grid_spec=pltpu.PrefetchScalarGridSpec(
            num_scalar_prefetch=1,
            grid=(2 * splits,),
            in_specs=[alone, alone, pl.BlockSpec((3, rows, width), lambda s, o: (0, 0, 0))]
            + weight_specs(depth, width, splits, 2),
            out_specs=[out, out],
            scratch_shapes=[pltpu.VMEM((3, rows, width), jnp.float32)],
        ),
        compiler_params=pltpu.CompilerParams(vmem_limit_bytes=16 << 20),
        cost_estimate=SMALL,
        name="project_peer",
    )(order, peer, peer_sibling, known, weight, weight, weight)


def taps_kernel(taps, forward, spectrum):
    for block in range(taps.shape[0] // BLOCK):
        spectrum[block] = jnp.dot(
            forward[...], taps[block * BLOCK : (block + 1) * BLOCK], preferred_element_type=jnp.float32
        )


def transform_taps(taps, forward):
    blocks, width = taps.shape[0] // BLOCK, taps.shape[1]
    return pl.pallas_call(
        taps_kernel,
        out_shape=jax.ShapeDtypeStruct((blocks, 2 * BLOCK, width), jnp.float32),
        compiler_params=pltpu.CompilerParams(vmem_limit_bytes=16 << 20),
        cost_estimate=SMALL,
        name="transform_taps",
    )(taps, forward)


def convolve_kernel(counts, *refs):
    n_source, n_query = counts
    sources = refs[:n_source]
    queries = refs[n_source : n_source + n_query]
    taps, forward, inverse, out, signal, spectrum, mixed = refs[n_source + n_query :]
    at = 0
    for source in sources:
        signal[at : at + source.shape[0]] = source[...]
        at += source.shape[0]
    n_blocks = at // BLOCK
    n_taps = taps.shape[0]
    n_out = n_blocks - n_taps
    for block in range(n_blocks):
        spectrum[block] = jnp.dot(
            forward[...], signal[block * BLOCK : (block + 1) * BLOCK], preferred_element_type=jnp.float32
        )
    half = BLOCK // 2
    rows = 8
    lanes = signal.shape[1]
    for sign, lane in [(sign, lane) for sign in (0, 1) for lane in range(0, signal.shape[1], lanes)]:

        def mix(turn, carry):
            base = pl.multiple_of(sign * half + turn * rows, rows)
            cos_at = pl.ds(base, rows), slice(lane, lane + lanes)
            sin_at = pl.ds(base + BLOCK, rows), slice(lane, lane + lanes)
            pairs = []
            for pair in range(n_blocks - 1):
                near_cos, near_sin = spectrum[pair, *cos_at], spectrum[pair, *sin_at]
                far_cos, far_sin = spectrum[pair + 1, *cos_at], spectrum[pair + 1, *sin_at]
                if sign == 0:
                    pairs.append((near_cos - far_sin, near_sin + far_cos))
                else:
                    pairs.append((near_cos + far_sin, near_sin - far_cos))
            for j in range(n_out):
                cos_sum = sin_sum = None
                for i in range(n_taps):
                    c, s = pairs[n_taps - 1 + j - i]
                    hc, hs = taps[i, *cos_at], taps[i, *sin_at]
                    cc, ss = c * hc - s * hs, c * hs + s * hc
                    cos_sum = cc if cos_sum is None else cos_sum + cc
                    sin_sum = ss if sin_sum is None else sin_sum + ss
                mixed[j, *cos_at] = cos_sum
                mixed[j, *sin_at] = sin_sum
            return carry

        lax.fori_loop(0, half // rows, mix, 0)
    convolved = [
        jnp.dot(inverse[...], mixed[j].astype(jnp.bfloat16), preferred_element_type=jnp.float32) for j in range(n_out)
    ]
    at = 0
    for query in queries:
        for row in range(0, query.shape[0], 32):
            block, offset = (at + row) // BLOCK, (at + row) % BLOCK
            out[at + row : at + row + 32] = (
                query[row : row + 32].astype(jnp.float32) * convolved[block][offset : offset + 32]
            ).astype(jnp.bfloat16)
        at += query.shape[0]


def convolve(sources, queries, taps, forward, inverse):
    length = sum(s.shape[0] for s in sources)
    rows = sum(q.shape[0] for q in queries)
    width = queries[0].shape[1]
    blocks = length // BLOCK
    outs = rows // BLOCK
    return pl.pallas_call(
        functools.partial(convolve_kernel, (len(sources), len(queries))),
        out_shape=jax.ShapeDtypeStruct((rows, width), jnp.bfloat16),
        scratch_shapes=[
            pltpu.VMEM((length, width), jnp.bfloat16),
            pltpu.VMEM((blocks, 2 * BLOCK, width), jnp.float32),
            pltpu.VMEM((outs, 2 * BLOCK, width), jnp.float32),
        ],
        compiler_params=pltpu.CompilerParams(vmem_limit_bytes=20 << 20),
        cost_estimate=SMALL,
        name="convolve",
    )(*sources, *queries, taps, forward, inverse)


def pair_taps(taps):
    other = lax.ppermute(taps, "ctx", [(i, i ^ 4) for i in range(32)])
    upper = (lax.axis_index("ctx") & 4) != 0
    return jnp.where(upper, jnp.stack([other, taps]), jnp.stack([taps, other]))


def exchange_taps(both):
    _, lags, width = both.shape
    groups = [[z * 8 + y * 4 + x for z in range(4) for x in range(4)] for y in range(2)]
    copies = jnp.broadcast_to(both[None], (16, 2, lags, width))
    every = lax.all_to_all(copies, "ctx", 0, 0, axis_index_groups=groups, tiled=True)
    return every.reshape(4, 4, 2, lags, width).transpose(0, 2, 1, 3, 4).reshape(-1, width)


def body(features, in_weight, filter_taps):
    peers = lax.axis_size("ctx")
    ahead = [[(i, i + by) for i in range(peers - by)] for by in (1, 2)]
    me = lax.axis_index("ch")
    order = jnp.stack([me, me ^ 1, me ^ 2, me ^ 3]).astype(jnp.int32)
    weight = jnp.transpose(in_weight, (1, 0, 2))
    forward, inverse = spectral_tables()

    have = {"features": features}

    def gate(name, needed):
        names = [name] + [n for n in needed if n != name]
        if len(names) > 1:
            for n, value in zip(names, lax.optimization_barrier([have[n] for n in names])):
                have[n] = value
        return have[name]

    have["both"] = pair_taps(filter_taps)
    have["sibling"] = lax.ppermute(features, "ch", SIBLING)
    for turn, (at, rows) in enumerate(CHUNKS):
        have["piece"] = gate("features", BEFORE_SEND[turn])[at : at + rows]
        have[f"arrived{turn}"] = lax.ppermute(gate("piece", BEFORE_START if turn == 0 else ()), "ch", PEER)

    have["taps"] = exchange_taps(have["both"])
    have["spectrum"] = transform_taps(have["taps"], forward)
    for turn, part in enumerate(project_own(order, have["features"], have["sibling"], weight)):
        have[f"known{turn}"] = part
    for turn in range(len(CHUNKS)):
        peer = gate(f"arrived{turn}", BEFORE_PASS[turn])
        peer_sibling = lax.ppermute(peer, "ch", SIBLING)
        known = have[f"known{turn}"]
        query, product = project_peer(order, peer, peer_sibling, known, weight)
        have[f"query{turn}"], have[f"product{turn}"] = query, product
        for number, group in enumerate(GROUPS):
            if group[-1] == turn:
                parts = [have[f"product{member}"] for member in group]
                together = jnp.concatenate(parts, 0) if len(parts) > 1 else parts[0]
                have[f"near{number}"] = lax.ppermute(together, "ctx", ahead[0])
                have[f"far{number}"] = lax.ppermute(together, "ctx", ahead[1])
    sources = [have[f"{side}{number}"] for side in ("far", "near") for number in range(len(GROUPS))]
    sources += [have[f"product{turn}"] for turn in range(len(CHUNKS))]
    queries = [have[f"query{turn}"] for turn in range(len(CHUNKS))]
    return convolve(sources, queries, have["spectrum"], forward, inverse)


def solution(mesh):
    in_specs = (P("ctx", "ch"), P(None, None, "ch"), P("ctx", "ch"))
    out_specs = P("ctx", "ch")
    return jax.shard_map(body, mesh=mesh, in_specs=in_specs, out_specs=out_specs, check_vma=False)
```

```python
import functools

import jax
import jax.numpy as jnp
import numpy as np
from jax import lax
from jax.experimental import pallas as pl
from jax.experimental.pallas import tpu as pltpu
from jax.sharding import PartitionSpec as P

BLOCK = 256
ROWS = 8
UNROLL = 16
WHOLE = pl.BlockSpec(memory_space=pltpu.VMEM)
SCALAR = pl.BlockSpec(memory_space=pltpu.SMEM)
SMALL = pl.CostEstimate(flops=1024, bytes_accessed=1024, transcendentals=0)
SIZES = (320, 384, 64)
CHUNKS = tuple((sum(SIZES[:turn]), size) for turn, size in enumerate(SIZES))
GROUPS = ((0, 1), (2,))
BEFORE_SEND = ((), ("sibling",), ("arrived0",))
BEFORE_PASS = (("taps",), ("product0", "spectrum"), ("product1",))
BEFORE_START = ("both",)
PEER = [(0, 2), (1, 3), (2, 0), (3, 1)]
SIBLING = [(0, 1), (1, 0), (2, 3), (3, 2)]


def spectral_tables():
    order = np.concatenate([np.arange(0, BLOCK, 2), np.arange(1, BLOCK, 2)])
    theta = np.pi * (2 * order + 1) / (2 * BLOCK)
    near = theta[:, None] * np.arange(BLOCK)[None, :]
    far = (np.arange(BLOCK) + BLOCK)[:, None] * theta[None, :]
    forward = np.concatenate([np.cos(near), np.sin(near)], 0)
    inverse = np.concatenate([np.cos(far), np.sin(far)], 1) / BLOCK
    return jnp.asarray(forward, jnp.bfloat16), jnp.asarray(inverse, jnp.bfloat16)


def weight_specs(depth, width, splits, first):
    return [
        pl.BlockSpec(
            (1, depth // splits, width),
            lambda s, o, kind=kind: (kind, o[first + s // splits] * splits + s % splits, 0),
        )
        for kind in range(3)
    ]


def project_own_kernel(order, own, sibling, *refs):
    weights, outs = refs[:3], refs[3:]
    step = pl.program_id(0)
    depth = weights[0].shape[1]
    splits = own.shape[1] // depth
    for turn in range(2 * splits):

        @pl.when(step == turn)
        def _():
            piece = (own, sibling)[turn // splits]
            columns = slice(turn % splits * depth, (turn % splits + 1) * depth)
            for kind, weight in enumerate(weights):
                at = 0
                for out in outs:
                    part = jnp.dot(
                        piece[at : at + out.shape[1], columns], weight[0], preferred_element_type=jnp.float32
                    )
                    out[kind] = part if turn == 0 else out[kind] + part
                    at += out.shape[1]


def project_own(order, features, sibling, weight):
    rows, depth = features.shape
    width = weight.shape[2]
    splits = 2
    alone = pl.BlockSpec((rows, depth), lambda s, o: (0, 0))
    return pl.pallas_call(
        project_own_kernel,
        out_shape=[jax.ShapeDtypeStruct((3, size, width), jnp.float32) for _, size in CHUNKS],
        grid_spec=pltpu.PrefetchScalarGridSpec(
            num_scalar_prefetch=1,
            grid=(2 * splits,),
            in_specs=[alone, alone] + weight_specs(depth, width, splits, 0),
            out_specs=[pl.BlockSpec((3, size, width), lambda s, o: (0, 0, 0)) for _, size in CHUNKS],
        ),
        compiler_params=pltpu.CompilerParams(vmem_limit_bytes=28 << 20),
        cost_estimate=SMALL,
        name="project_own",
    )(order, features, sibling, weight, weight, weight)


def project_peer_kernel(order, peer, peer_sibling, known, *refs):
    weights, (query, product, total) = refs[:3], refs[3:]
    step = pl.program_id(0)
    depth = weights[0].shape[1]
    splits = peer.shape[1] // depth
    for turn in range(2 * splits):

        @pl.when(step == turn)
        def _():
            piece = (peer, peer_sibling)[turn // splits]
            columns = slice(turn % splits * depth, (turn % splits + 1) * depth)
            full = []
            for kind, weight in enumerate(weights):
                part = jnp.dot(piece[:, columns], weight[0], preferred_element_type=jnp.float32)
                full.append(part + (known[kind] if turn == 0 else total[kind]))
            if turn < 2 * splits - 1:
                for kind in range(3):
                    total[kind] = full[kind]
            else:
                query[...] = full[0].astype(jnp.bfloat16)
                product[...] = (full[1] * full[2]).astype(jnp.bfloat16)


def project_peer(order, peer, peer_sibling, known, weight):
    rows, depth = peer.shape
    width = weight.shape[2]
    splits = 2
    alone = pl.BlockSpec((rows, depth), lambda s, o: (0, 0))
    out = pl.BlockSpec((rows, width), lambda s, o: (0, 0))
    return pl.pallas_call(
        project_peer_kernel,
        out_shape=[jax.ShapeDtypeStruct((rows, width), jnp.bfloat16)] * 2,
        grid_spec=pltpu.PrefetchScalarGridSpec(
            num_scalar_prefetch=1,
            grid=(2 * splits,),
            in_specs=[alone, alone, pl.BlockSpec((3, rows, width), lambda s, o: (0, 0, 0))]
            + weight_specs(depth, width, splits, 2),
            out_specs=[out, out],
            scratch_shapes=[pltpu.VMEM((3, rows, width), jnp.float32)],
        ),
        compiler_params=pltpu.CompilerParams(vmem_limit_bytes=16 << 20),
        cost_estimate=SMALL,
        name="project_peer",
    )(order, peer, peer_sibling, known, weight, weight, weight)


def taps_kernel(taps, forward, spectrum):
    for block in range(taps.shape[0] // BLOCK):
        spectrum[block] = jnp.dot(
            forward[...], taps[block * BLOCK : (block + 1) * BLOCK], preferred_element_type=jnp.float32
        )


def transform_taps(taps, forward):
    blocks, width = taps.shape[0] // BLOCK, taps.shape[1]
    return pl.pallas_call(
        taps_kernel,
        out_shape=jax.ShapeDtypeStruct((blocks, 2 * BLOCK, width), jnp.float32),
        compiler_params=pltpu.CompilerParams(vmem_limit_bytes=16 << 20),
        cost_estimate=SMALL,
        name="transform_taps",
    )(taps, forward)


def convolve_kernel(counts, *refs):
    n_source, n_query = counts
    sources = refs[:n_source]
    queries = refs[n_source : n_source + n_query]
    taps, forward, inverse, out, signal, spectrum, mixed = refs[n_source + n_query :]
    at = 0
    for source in sources:
        signal[at : at + source.shape[0]] = source[...]
        at += source.shape[0]
    n_blocks = at // BLOCK
    n_taps = taps.shape[0]
    n_out = n_blocks - n_taps
    for block in range(n_blocks):
        spectrum[block] = jnp.dot(
            forward[...], signal[block * BLOCK : (block + 1) * BLOCK], preferred_element_type=jnp.float32
        )
    half = BLOCK // 2
    rows = ROWS
    lanes = signal.shape[1]
    for sign, lane in [(sign, lane) for sign in (0, 1) for lane in range(0, signal.shape[1], lanes)]:

        def mix(turn, carry):
            base = pl.multiple_of(sign * half + turn * rows, rows)
            cos_at = pl.ds(base, rows), slice(lane, lane + lanes)
            sin_at = pl.ds(base + BLOCK, rows), slice(lane, lane + lanes)
            pairs = []
            for pair in range(n_blocks - 1):
                near_cos, near_sin = spectrum[pair, *cos_at], spectrum[pair, *sin_at]
                far_cos, far_sin = spectrum[pair + 1, *cos_at], spectrum[pair + 1, *sin_at]
                if sign == 0:
                    pairs.append((near_cos - far_sin, near_sin + far_cos))
                else:
                    pairs.append((near_cos + far_sin, near_sin - far_cos))
            for j in range(n_out):
                cos_sum = sin_sum = None
                for i in range(n_taps):
                    c, s = pairs[n_taps - 1 + j - i]
                    hc, hs = taps[i, *cos_at], taps[i, *sin_at]
                    cc, ss = c * hc - s * hs, c * hs + s * hc
                    cos_sum = cc if cos_sum is None else cos_sum + cc
                    sin_sum = ss if sin_sum is None else sin_sum + ss
                mixed[j, *cos_at] = cos_sum
                mixed[j, *sin_at] = sin_sum
            return carry

        lax.fori_loop(0, half // rows, mix, 0, unroll=UNROLL)
    convolved = [
        jnp.dot(inverse[...], mixed[j].astype(jnp.bfloat16), preferred_element_type=jnp.float32) for j in range(n_out)
    ]
    at = 0
    for query in queries:
        for row in range(0, query.shape[0], 32):
            block, offset = (at + row) // BLOCK, (at + row) % BLOCK
            out[at + row : at + row + 32] = (
                query[row : row + 32].astype(jnp.float32) * convolved[block][offset : offset + 32]
            ).astype(jnp.bfloat16)
        at += query.shape[0]


def convolve(sources, queries, taps, forward, inverse):
    length = sum(s.shape[0] for s in sources)
    rows = sum(q.shape[0] for q in queries)
    width = queries[0].shape[1]
    blocks = length // BLOCK
    outs = rows // BLOCK
    return pl.pallas_call(
        functools.partial(convolve_kernel, (len(sources), len(queries))),
        out_shape=jax.ShapeDtypeStruct((rows, width), jnp.bfloat16),
        scratch_shapes=[
            pltpu.VMEM((length, width), jnp.bfloat16),
            pltpu.VMEM((blocks, 2 * BLOCK, width), jnp.float32),
            pltpu.VMEM((outs, 2 * BLOCK, width), jnp.float32),
        ],
        compiler_params=pltpu.CompilerParams(vmem_limit_bytes=20 << 20),
        cost_estimate=SMALL,
        name="convolve",
    )(*sources, *queries, taps, forward, inverse)


def pair_taps(taps):
    other = lax.ppermute(taps, "ctx", [(i, i ^ 4) for i in range(32)])
    upper = (lax.axis_index("ctx") & 4) != 0
    return jnp.where(upper, jnp.stack([other, taps]), jnp.stack([taps, other]))


def exchange_taps(both):
    _, lags, width = both.shape
    groups = [[z * 8 + y * 4 + x for z in range(4) for x in range(4)] for y in range(2)]
    copies = jnp.broadcast_to(both[None], (16, 2, lags, width))
    every = lax.all_to_all(copies, "ctx", 0, 0, axis_index_groups=groups, tiled=True)
    return every.reshape(4, 4, 2, lags, width).transpose(0, 2, 1, 3, 4).reshape(-1, width)


def body(features, in_weight, filter_taps):
    peers = lax.axis_size("ctx")
    ahead = [[(i, i + by) for i in range(peers - by)] for by in (1, 2)]
    me = lax.axis_index("ch")
    order = jnp.stack([me, me ^ 1, me ^ 2, me ^ 3]).astype(jnp.int32)
    weight = jnp.transpose(in_weight, (1, 0, 2))
    forward, inverse = spectral_tables()

    have = {"features": features}

    def gate(name, needed):
        names = [name] + [n for n in needed if n != name]
        if len(names) > 1:
            for n, value in zip(names, lax.optimization_barrier([have[n] for n in names])):
                have[n] = value
        return have[name]

    have["both"] = pair_taps(filter_taps)
    have["sibling"] = lax.ppermute(features, "ch", SIBLING)
    for turn, (at, rows) in enumerate(CHUNKS):
        have["piece"] = gate("features", BEFORE_SEND[turn])[at : at + rows]
        have[f"arrived{turn}"] = lax.ppermute(gate("piece", BEFORE_START if turn == 0 else ()), "ch", PEER)

    have["taps"] = exchange_taps(have["both"])
    have["spectrum"] = transform_taps(have["taps"], forward)
    for turn, part in enumerate(project_own(order, have["features"], have["sibling"], weight)):
        have[f"known{turn}"] = part
    for turn in range(len(CHUNKS)):
        peer = gate(f"arrived{turn}", BEFORE_PASS[turn])
        peer_sibling = lax.ppermute(peer, "ch", SIBLING)
        known = have[f"known{turn}"]
        query, product = project_peer(order, peer, peer_sibling, known, weight)
        have[f"query{turn}"], have[f"product{turn}"] = query, product
        for number, group in enumerate(GROUPS):
            if group[-1] == turn:
                parts = [have[f"product{member}"] for member in group]
                together = jnp.concatenate(parts, 0) if len(parts) > 1 else parts[0]
                have[f"near{number}"] = lax.ppermute(together, "ctx", ahead[0])
                have[f"far{number}"] = lax.ppermute(together, "ctx", ahead[1])
    sources = [have[f"{side}{number}"] for side in ("far", "near") for number in range(len(GROUPS))]
    sources += [have[f"product{turn}"] for turn in range(len(CHUNKS))]
    queries = [have[f"query{turn}"] for turn in range(len(CHUNKS))]
    return convolve(sources, queries, have["spectrum"], forward, inverse)


def solution(mesh):
    in_specs = (P("ctx", "ch"), P(None, None, "ch"), P("ctx", "ch"))
    out_specs = P("ctx", "ch")
    return jax.shard_map(body, mesh=mesh, in_specs=in_specs, out_specs=out_specs, check_vma=False)
```
